32 devices in a mesh: row: 8 (over y, x, core), col: 4 (over z).
Axes of the slice: x: 2, y: 2, z: 4, core: 2. Of those that a mesh axis runs over, the one named last changes fastest.
Arguments:
- rhs: float32 [4, 2048, 1024], P(None, 'row', 'col'), may hold values from -6 to 6
- l_panel: bfloat16 [4, 2048, 16384], P(None, 'row', 'col'), may hold values from -0.046875 to 0.046875
- x_solved: bfloat16 [16384, 1024], P('col'), may hold values from -6 to 6
- diag_inv: bfloat16 [4, 2048, 2048], P(None, 'row'), may hold values from -1 to 1.5, as said below
- l_inner: bfloat16 [6, 2048, 2048], P(None, 'row'), may hold values from -0.0625 to 0.0625
Outputs:
- x_window: float32 [4, 2048, 1024], P(None, 'row', 'col')
The draws below stay inside these ranges and needn't reach their ends.
Inputs may be any that keep to these rules, and one draw needn't show every extreme that they name: `diag_inv`: each block is lower triangular with diagonal entries between one half and three halves.
All inputs are finite; a program needn't handle non-finite values.
Results may differ from the reference program's by a relative error of at most 0.0045.
Values may be sent and summed in bfloat16 or wider, within the bound.
No kernel may reach another device: no remote copies, remote signals or barrier semaphores. Data moves between devices by JAX's collectives and lax.ppermute only.
A program may use at most 64 MiB of HBM per device.

```python
import math
import jax
import jax.numpy as jnp
from jax import lax

NRHS = 1024
BLK = 2048
STEPS = 4
SOLVED = 16384
PAIRS = 6


def draw_diag_inv(key, part):
    key_diag, key_off = jax.random.split(jax.random.fold_in(key, 11))
    shape = (STEPS, BLK, BLK)
    row_ids = lax.broadcasted_iota(jnp.int32, shape, 1)
    col_ids = lax.broadcasted_iota(jnp.int32, shape, 2)
    diagonal = jax.random.uniform(key_diag, shape, jnp.float32, 0.6, 1.4)
    lower = jnp.clip(jax.random.normal(key_off, shape, jnp.float32), -4.0, 4.0) * (0.6 / math.sqrt(BLK))
    values = jnp.where(row_ids == col_ids, diagonal, jnp.where(col_ids < row_ids, lower, 0.0))
    return values.astype(jnp.bfloat16)


def raised(result, key, source, target, blocks, factor):
    owner, partner = [(jnp.arange(result.shape[position]) // (result.shape[position] // blocks)).reshape([-1 if axis == position else 1 for axis in range(result.ndim)]) for position in (source, target)]
    chosen = jax.random.permutation(key, blocks)[partner]
    strong = (owner == chosen) | (owner == (partner + blocks // 2) % blocks)
    return jnp.where(strong, factor * result, result)


def block_scale(own_key, shape, pieces, smallest, top_value):
    gain, own = 1.0, jax.random.fold_in(own_key, 6)
    for dim, blocks in pieces:
        heights = jnp.exp(jax.random.uniform(jax.random.fold_in(own, dim), (blocks,), jnp.float32, smallest / len(pieces), top_value / len(pieces)))
        gain = gain * jnp.repeat(heights, shape[dim] // blocks).reshape([-1 if axis == dim else 1 for axis in range(len(shape))])
    return gain


def noise(key, shape, scale, bound, pieces=(), dtype=jnp.bfloat16):
    level = block_scale(key, shape, pieces, -0.22, 0.18) if pieces else 1.0
    result = jax.random.normal(key, shape, jnp.float32) * scale * level
    return jnp.minimum(jnp.maximum(result, -bound), bound).astype(dtype)


def noise_with(rng, dims, deviation, bound, pieces, heavy, dtype=jnp.bfloat16):
    entries = deviation * jax.random.normal(rng, dims, jnp.float32)
    if pieces:
        entries = entries * block_scale(rng, dims, pieces, -0.22, 0.18)
    return jnp.clip(raised(entries, jax.random.fold_in(rng, 3), *heavy), -bound, bound).astype(dtype)


def setup_inputs(seed: int = 0) -> dict:
    streams_of = jax.random.split(jax.random.key(seed), 6)
    return {
        "rhs": noise(streams_of[0], (STEPS, BLK, NRHS), 1.0, 6.0, ((1, 8), (2, 4)), jnp.float32),
        "l_panel": noise(streams_of[1], (STEPS, BLK, SOLVED), SOLVED ** -0.5, 0.046875, ((1, 8), (2, 4))),
        "x_solved": noise_with(streams_of[2], (SOLVED, NRHS), 1.0, 6.0, ((0, 4),), (0, 1, 4, 2.0)),
        "diag_inv": draw_diag_inv(jax.random.fold_in(streams_of[5], 71), 0),
        "l_inner": noise(streams_of[4], (PAIRS, BLK, BLK), (4 * BLK) ** -0.5, 0.0625, ((1, 8),)),
    }


def reference(rhs, l_panel, x_solved, diag_inv, l_inner):
    solved_low = []
    results = []
    for target in range(STEPS):
        products = jnp.dot(l_panel[target], x_solved, preferred_element_type=jnp.float32)
        resid = rhs[target] - products
        for earlier in range(target):
            resid = resid - jnp.dot(l_inner[target * (target - 1) // 2 + earlier], solved_low[earlier], preferred_element_type=jnp.float32)
        current = jnp.dot(diag_inv[target], resid.astype(jnp.bfloat16), preferred_element_type=jnp.float32)
        results.append(current)
        solved_low.append(current.astype(jnp.bfloat16))
    return jnp.stack(results, axis=0)
```

```python
import functools

import jax
import jax.numpy as jnp
from jax import lax
from jax.experimental import pallas as pl
from jax.experimental.pallas import tpu as pltpu
from jax.sharding import PartitionSpec as P

F32, BF16 = jnp.float32, jnp.bfloat16


def inner_index(target, earlier):
    return target * (target - 1) // 2 + earlier


def product_kernel(l_ref, x_ref, out_ref):
    out_ref[...] = jnp.dot(l_ref[...], x_ref[...], preferred_element_type=F32)


def panel_product(l_block, x_solved, width):
    rows, depth = l_block.shape
    total = x_solved.shape[1]
    return pl.pallas_call(
        product_kernel,
        grid=(total // width,),
        in_specs=[
            pl.BlockSpec((rows, depth), lambda i: (0, 0)),
            pl.BlockSpec((depth, width), lambda i: (0, i)),
        ],
        out_specs=pl.BlockSpec((rows, width), lambda i: (0, i)),
        out_shape=jax.ShapeDtypeStruct((rows, total), F32),
        compiler_params=pltpu.CompilerParams(vmem_limit_bytes=40 << 20),
        cost_estimate=pl.CostEstimate(
            flops=2 * rows * depth * total,
            bytes_accessed=2 * (rows + total) * depth + 4 * rows * total,
            transcendentals=0,
        ),
    )(l_block, x_solved)


def apply_kernel(parts, subtract, low, place_ref, *refs):
    own_ref, other_ref = refs[0], refs[1]
    shards = refs[2 : 2 + parts]
    pending_ref = refs[2 + parts] if subtract else None
    outs = refs[2 + parts + (1 if subtract else 0) :]
    rows, high = own_ref.shape[0], 2 * own_ref.shape[0]
    for ref, offset in ((own_ref, place_ref[0]), (other_ref, place_ref[1])):
        there = pl.ds(pl.multiple_of(offset, rows), rows)
        total = jnp.zeros((rows, shards[0].shape[1]), F32)
        entry = 0
        for shard in shards:
            for piece in range(shard.shape[0] // high):
                begin = pl.multiple_of(place_ref[2 + entry], high)
                total += jnp.dot(
                    ref[:, pl.ds(begin, high)],
                    shard[piece * high : (piece + 1) * high, :],
                    preferred_element_type=F32,
                )
                entry += 1
        if subtract:
            total = pending_ref[there, :] - total
        outs[0][there, :] = total
        if low:
            outs[1][there, :] = total.astype(BF16)


def apply_rows(place, own, other, shards, pending, low):
    high, width = shards[0].shape
    flops = 4 * own.shape[0] * own.shape[1] * width
    shapes = [jax.ShapeDtypeStruct((high, width), F32)]
    if low:
        shapes.append(jax.ShapeDtypeStruct((high, width), BF16))
    operands = [own, other, *shards] + ([] if pending is None else [pending])
    return pl.pallas_call(
        functools.partial(apply_kernel, len(shards), pending is not None, low),
        in_specs=[pl.BlockSpec(memory_space=pltpu.SMEM)]
        + [pl.BlockSpec(memory_space=pltpu.VMEM)] * len(operands),
        out_specs=[pl.BlockSpec(memory_space=pltpu.VMEM)] * len(shapes),
        out_shape=shapes,
        compiler_params=pltpu.CompilerParams(vmem_limit_bytes=16 << 20),
        cost_estimate=pl.CostEstimate(
            flops=flops, bytes_accessed=4 * own.size + 4 * high * width, transcendentals=0
        ),
    )(place, *operands)


def local(rhs, l_panel, x_solved, diag_inv, l_inner, row_count, col_count):
    steps, rows, _ = l_panel.shape
    width = rhs.shape[2]
    half = width // 2
    high = 2 * rows
    me, place_col = lax.axis_index("row"), lax.axis_index("col")
    core, chip = me % 2, me // 2
    bits = [1 << k for k in range((row_count // 2 - 1).bit_length())]
    orders = (bits, bits[::-1])

    def masks(order):
        found = [0]
        for bit in order:
            found += [mask ^ bit for mask in found]
        return found

    first, second = (jnp.array(masks(order), jnp.int32) for order in orders)
    shard_chip = chip ^ jnp.where(core == 0, first, second)
    place = jnp.concatenate(
        [jnp.stack([core * rows, (1 - core) * rows]), shard_chip * high]
    ).astype(jnp.int32)

    def swap(value):
        return lax.ppermute(value, "row", [(i, i ^ 1) for i in range(row_count)])

    def gather(value):
        shards = [value]
        for stage in range(len(bits)):
            pairs = [(i, i ^ (2 * orders[i % 2][stage])) for i in range(row_count)]
            send = shards[0] if stage == 0 else jnp.concatenate(shards, axis=0)
            shards.append(lax.ppermute(send, "row", pairs))
        return shards

    def chunk(block, index):
        return lax.dynamic_slice_in_dim(block, jnp.clip(index, 0, col_count - 1) * width, width, 1)

    def reduce_block(block):
        up = down = None
        for step in range(col_count - 1):
            high_chunk = chunk(block, place_col + col_count - 1 - step)
            low_chunk = chunk(block, place_col - col_count + 1 + step)
            if step:
                high_chunk += up.astype(F32)
                low_chunk += down.astype(F32)
            pairs = [(i, i + 1) for i in range(step + 1)]
            up = lax.ppermute(high_chunk.astype(BF16), "col", pairs)
            last = col_count - 1
            down = lax.ppermute(
                low_chunk.astype(BF16), "col", [(last - i, last - j) for i, j in pairs]
            )
        return up.astype(F32) + down.astype(F32) + chunk(block, place_col)

    def to_halves(value):
        mine = lax.dynamic_slice_in_dim(value, core * half, half, 1)
        other = swap(lax.dynamic_slice_in_dim(value, (1 - core) * half, half, 1))
        return jnp.where(
            core == 0,
            jnp.concatenate([mine, other], axis=0),
            jnp.concatenate([other, mine], axis=0),
        )

    def from_halves(value):
        mine = lax.dynamic_slice_in_dim(value, core * rows, rows, 0)
        other = swap(lax.dynamic_slice_in_dim(value, (1 - core) * rows, rows, 0))
        return jnp.where(
            core == 0,
            jnp.concatenate([mine, other], axis=1),
            jnp.concatenate([other, mine], axis=1),
        )

    pending = []
    for target in range(steps):
        block = panel_product(l_panel[target], x_solved, width)
        pending.append(to_halves(rhs[target] - reduce_block(block)))
    diag_other = [swap(diag_inv[target]) for target in range(steps)]
    inner_other = {}
    for earlier in range(steps):
        for target in range(earlier + 1, steps):
            index = inner_index(target, earlier)
            inner_other[index] = swap(l_inner[index])
    results = []
    resid_low = pending[0].astype(BF16)
    for target in range(steps):
        last = target + 1 == steps
        current = apply_rows(
            place, diag_inv[target], diag_other[target], gather(resid_low), None, not last
        )
        results.append(from_halves(current[0]))
        if last:
            break
        shards = gather(current[1])
        for follower in range(target + 1, steps):
            index = inner_index(follower, target)
            updated = apply_rows(
                place, l_inner[index], inner_other[index], shards, pending[follower], follower == target + 1
            )
            pending[follower] = updated[0]
            if follower == target + 1:
                resid_low = updated[1]
    return jnp.stack(results, axis=0)


def solution(mesh):
    in_specs = (
        P(None, "row", "col"),
        P(None, "row", "col"),
        P("col", None),
        P(None, "row", None),
        P(None, "row", None),
    )
    out_specs = P(None, "row", "col")
    body = functools.partial(
        local, row_count=mesh.shape["row"], col_count=mesh.shape["col"]
    )
    return jax.shard_map(body, mesh=mesh, in_specs=in_specs, out_specs=out_specs, check_vma=False)
```

```python
import functools

import jax
import jax.numpy as jnp
from jax import lax
from jax.experimental import pallas as pl
from jax.experimental.pallas import tpu as pltpu
from jax.sharding import PartitionSpec as P

F32, BF16 = jnp.float32, jnp.bfloat16
VMEM = pl.BlockSpec(memory_space=pltpu.VMEM)
SMEM = pl.BlockSpec(memory_space=pltpu.SMEM)
ANY = pl.BlockSpec(memory_space=pl.ANY)


def inner_index(target, earlier):
    return target * (target - 1) // 2 + earlier


def product_kernel(blocks, count, place_ref, *refs):
    l_refs, x_ref, outs = refs[:blocks], refs[blocks], refs[blocks + 1 :]
    for turn in range(count):

        @pl.when(pl.program_id(0) == turn)
        def _():
            for block in range(blocks):
                out = outs[block * count + turn]
                out[...] = jnp.dot(
                    l_refs[block][...], x_ref[...], preferred_element_type=F32
                ).astype(out.dtype)


def panel_products(place, l_panel, x_solved, targets, width):
    _, rows, depth = l_panel.shape
    count = x_solved.shape[1] // width
    types = [BF16] * (count - 1) + [F32]
    found = pl.pallas_call(
        functools.partial(product_kernel, len(targets), count),
        grid_spec=pltpu.PrefetchScalarGridSpec(
            num_scalar_prefetch=1,
            grid=(count,),
            in_specs=[
                pl.BlockSpec((None, rows, depth), lambda i, place, t=t: (t, 0, 0)) for t in targets
            ]
            + [pl.BlockSpec((depth, width), lambda i, place: (0, place[i]))],
            out_specs=[pl.BlockSpec((rows, width), lambda i, place: (0, 0))]
            * (count * len(targets)),
        ),
        out_shape=[jax.ShapeDtypeStruct((rows, width), t) for t in types] * len(targets),
        compiler_params=pltpu.CompilerParams(vmem_limit_bytes=40 << 20),
        cost_estimate=pl.CostEstimate(
            flops=2 * rows * depth * x_solved.shape[1] * len(targets),
            bytes_accessed=2 * (rows * len(targets) + x_solved.shape[1]) * depth,
            transcendentals=0,
        ),
    )(place, *[l_panel] * len(targets), x_solved)
    return [found[i * count : (i + 1) * count] for i in range(len(targets))]


def load_kernel(index, place_ref, own_ref, other_ref, out_ref, sems):
    rows = own_ref.shape[1]
    copies = [
        pltpu.make_async_copy(
            ref.at[index],
            out_ref.at[pl.ds(pl.multiple_of(place_ref[k], rows), rows)],
            sems.at[k],
        )
        for k, ref in enumerate((own_ref, other_ref))
    ]
    for copy in copies:
        copy.start()
    for copy in copies:
        copy.wait()


def load_rows(place, own, other, index):
    _, rows, depth = own.shape
    return pl.pallas_call(
        functools.partial(load_kernel, index),
        in_specs=[SMEM, ANY, ANY],
        out_specs=VMEM,
        out_shape=jax.ShapeDtypeStruct((2 * rows, depth), own.dtype),
        scratch_shapes=[pltpu.SemaphoreType.DMA((2,))],
        compiler_params=pltpu.CompilerParams(vmem_limit_bytes=8 << 20),
        cost_estimate=pl.CostEstimate(
            flops=0, bytes_accessed=8 * rows * depth, transcendentals=0
        ),
    )(place, own, other)


def apply_kernel(parts, subtract, types, place_ref, matrix_ref, *refs):
    shards = refs[:parts]
    outs = refs[parts + subtract :]
    high, width = shards[0].shape
    total = jnp.zeros((high, width), F32)
    for entry, shard in enumerate(shards):
        begin = pl.multiple_of(place_ref[2 + entry], high)
        total += jnp.dot(
            matrix_ref[:, pl.ds(begin, high)], shard[...], preferred_element_type=F32
        )
    if subtract:
        total = refs[parts][...] - total
    for out in outs:
        out[...] = total.astype(out.dtype)


def apply_rows(place, matrix, shards, pending, types):
    high, width = shards[0].shape
    operands = [matrix, *shards] + ([] if pending is None else [pending])
    return pl.pallas_call(
        functools.partial(apply_kernel, len(shards), int(pending is not None), types),
        in_specs=[SMEM] + [VMEM] * len(operands),
        out_specs=[VMEM] * len(types),
        out_shape=[jax.ShapeDtypeStruct((high, width), t) for t in types],
        compiler_params=pltpu.CompilerParams(vmem_limit_bytes=16 << 20),
        cost_estimate=pl.CostEstimate(
            flops=4 * matrix.size * width, bytes_accessed=2 * matrix.size, transcendentals=0
        ),
    )(place, *operands)


def local(rhs, l_panel, x_solved, diag_inv, l_inner, row_count, col_count):
    steps, rows, _ = l_panel.shape
    width = rhs.shape[2]
    half = width // 2
    high = 2 * rows
    chips = row_count // 2
    me, mine = lax.axis_index("row"), lax.axis_index("col")
    core, chip = me % 2, me // 2
    order = jnp.arange(chips, dtype=jnp.int32)
    place = jnp.concatenate(
        [jnp.stack([core * rows, (1 - core) * rows]), (chip ^ order) * high]
    ).astype(jnp.int32)
    turns = (mine + 1 + jnp.arange(col_count, dtype=jnp.int32)) % col_count

    def swap(value):
        return lax.ppermute(value, "row", [(i, i ^ 1) for i in range(row_count)])

    def gather(value):
        far = [
            lax.ppermute(value, "row", [(i, i ^ (2 * mask)) for i in range(row_count)])
            for mask in range(1, chips)
        ]
        return [value, *far]

    def send_chunks(chunks):
        return [
            lax.ppermute(
                chunks[turn], "col", [(i, (i + turn + 1) % col_count) for i in range(col_count)]
            )
            for turn in range(col_count - 1)
        ]

    def reduced(target, chunks, arrived):
        total = chunks[-1]
        for part in arrived:
            total = total + part.astype(F32)
        return rhs[target] - total

    def to_halves(value):
        kept = lax.dynamic_slice_in_dim(value, core * half, half, 1)
        other = swap(lax.dynamic_slice_in_dim(value, (1 - core) * half, half, 1))
        return jnp.where(
            core == 0,
            jnp.concatenate([kept, other], axis=0),
            jnp.concatenate([other, kept], axis=0),
        )

    def from_halves(value):
        kept = lax.dynamic_slice_in_dim(value, core * rows, rows, 0)
        other = swap(lax.dynamic_slice_in_dim(value, (1 - core) * rows, rows, 0))
        return jnp.where(
            core == 0,
            jnp.concatenate([kept, other], axis=1),
            jnp.concatenate([other, kept], axis=1),
        )

    diag_other = swap(diag_inv)
    chunks = panel_products(turns, l_panel, x_solved, [0], width)
    arrived = send_chunks(chunks[0])
    if steps > 1:
        chunks += panel_products(turns, l_panel, x_solved, range(1, steps), width)
    l_inner, diag_other = lax.optimization_barrier((l_inner, diag_other))
    inner_other = swap(l_inner)
    pending = [to_halves(reduced(0, chunks[0], arrived))]
    for target in range(1, steps):
        sent, arrived = lax.optimization_barrier((chunks[target][:-1], arrived))
        arrived = send_chunks(sent)
        pending.append(to_halves(reduced(target, chunks[target], arrived)))
    results = []
    resid_low = pending[0].astype(BF16)
    for target in range(steps):
        last = target + 1 == steps
        matrix = load_rows(place, diag_inv, diag_other, target)
        current = apply_rows(place, matrix, gather(resid_low), None, (F32,) if last else (F32, BF16))
        results.append(from_halves(current[0]))
        if last:
            break
        shards = gather(current[1])
        for follower in range(target + 1, steps):
            index = inner_index(follower, target)
            matrix = load_rows(place, l_inner, inner_other, index)
            following = follower == target + 1
            updated = apply_rows(
                place, matrix, shards, pending[follower], (BF16,) if following else (F32,)
            )
            if following:
                resid_low = updated[0]
            else:
                pending[follower] = updated[0]
    return jnp.stack(results, axis=0)


def solution(mesh):
    in_specs = (
        P(None, "row", "col"),
        P(None, "row", "col"),
        P("col", None),
        P(None, "row", None),
        P(None, "row", None),
    )
    out_specs = P(None, "row", "col")
    body = functools.partial(local, row_count=mesh.shape["row"], col_count=mesh.shape["col"])
    return jax.shard_map(body, mesh=mesh, in_specs=in_specs, out_specs=out_specs, check_vma=False)
```

```python
import functools

import jax
import jax.numpy as jnp
from jax import lax
from jax.experimental import pallas as pl
from jax.experimental.pallas import tpu as pltpu
from jax.sharding import PartitionSpec as P

F32, BF16 = jnp.float32, jnp.bfloat16
VMEM = pl.BlockSpec(memory_space=pltpu.VMEM)
HBM = pl.BlockSpec(memory_space=pltpu.HBM)
SMALL = pl.CostEstimate(flops=1024, bytes_accessed=1024, transcendentals=0)


def inner_index(target, earlier):
    return target * (target - 1) // 2 + earlier


def params(mebibytes):
    return pltpu.CompilerParams(vmem_limit_bytes=mebibytes << 20)


def work(rows, depth, columns):
    return pl.CostEstimate(
        flops=2 * rows * depth * columns,
        bytes_accessed=2 * (rows + columns) * depth,
        transcendentals=0,
    )


def accumulate(total, piece, part, there=slice(None)):
    if piece == 0:
        total[:, there] = part
    else:
        total[:, there] += part


def first_kernel(shifts, pieces, l_ref, x_ref, *refs):
    count = len(shifts)
    outs, (l_buf, x_buf, total, l_sems, x_sems) = refs[:count], refs[count:]
    deep = x_ref.shape[0] // pieces
    width = x_ref.shape[1] // count
    mine = lax.axis_index("col")
    l_copies, x_copies = [], []
    for piece in range(pieces):
        cut = pl.ds(piece * deep, deep)
        l_copies.append(
            pltpu.make_async_copy(l_ref.at[0, :, cut], l_buf.at[piece], l_sems.at[piece])
        )
        x_copies.append(pltpu.make_async_copy(x_ref.at[cut], x_buf.at[piece], x_sems.at[piece]))
    for piece in range(pieces):
        l_copies[piece].start()
        x_copies[piece].start()
    for piece in range(pieces):
        l_copies[piece].wait()
        x_copies[piece].wait()
        accumulate(
            total, piece, jnp.dot(l_buf[piece], x_buf[piece], preferred_element_type=F32)
        )
    for shift, out in zip(shifts, outs):
        begin = pl.multiple_of(lax.rem(mine + shift, count) * width, width)
        out[...] = total[:, pl.ds(begin, width)].astype(out.dtype)


def second_kernel(shifts, pieces, flight, l_ref, x_ref, *refs):
    count = len(shifts)
    rows, depth = l_ref.shape[1:]
    blocks = l_ref.shape[0] - 1
    outs, refs = refs[: blocks * count], refs[blocks * count :]
    l_buf, x_buf, total, sent, kept, l_sems, x_sems, out_sems = refs
    deep = depth // pieces
    width = x_ref.shape[1] // count
    mine = lax.axis_index("col")
    copies = []
    for piece in range(pieces):
        cut = pl.ds(piece * deep, deep)
        copies.append(
            [
                pltpu.make_async_copy(
                    l_ref.at[block + 1, :, cut],
                    l_buf.at[piece, pl.ds(block * rows, rows)],
                    l_sems.at[piece, block],
                )
                for block in range(blocks)
            ]
            + [pltpu.make_async_copy(x_ref.at[cut], x_buf.at[piece], x_sems.at[piece])]
        )
    for row in copies[:flight]:
        for copy in row:
            copy.start()
    for piece in range(pieces):
        for copy in copies[piece]:
            copy.wait()
        if piece + flight < pieces:
            for copy in copies[piece + flight]:
                copy.start()
        accumulate(
            total, piece, jnp.dot(l_buf[piece], x_buf[piece], preferred_element_type=F32)
        )
    copies = []
    for block in range(blocks):
        for k, shift in enumerate(shifts):
            begin = pl.multiple_of(lax.rem(mine + shift, count) * width, width)
            found = total[block * rows : (block + 1) * rows, pl.ds(begin, width)]
            held = sent.at[block, k] if shift else kept.at[block]
            held[...] = found.astype(held.dtype)
            copy = pltpu.make_async_copy(held, outs[block * count + k], out_sems.at[block, k])
            copy.start()
            copies.append(copy)
    for copy in copies:
        copy.wait()


def load_kernel(indices, *refs):
    count = len(refs) // 2
    ins, outs, sems = refs[:count], refs[count:-1], refs[-1]
    copies = [
        pltpu.make_async_copy(ref.at[index], out.at[place], sems.at[k, place])
        for k, (ref, out) in enumerate(zip(ins, outs))
        for place, index in enumerate(indices)
    ]
    for copy in copies:
        copy.start()
    for copy in copies:
        copy.wait()


def load(arrays, indices):
    shapes = [
        jax.ShapeDtypeStruct((len(indices), *array.shape[1:]), array.dtype) for array in arrays
    ]
    return pl.pallas_call(
        functools.partial(load_kernel, tuple(indices)),
        in_specs=[HBM] * len(arrays),
        out_specs=[VMEM] * len(arrays),
        out_shape=shapes,
        scratch_shapes=[pltpu.SemaphoreType.DMA((len(arrays), len(indices)))],
        compiler_params=params(16),
        cost_estimate=SMALL,
    )(*arrays)


def reduce_kernel(parts, rhs_ref, own_ref, *refs):
    arrived, refs = refs[:parts], refs[parts:]
    taken, (kept_ref, other_ref) = refs[:-2], refs[-2:]
    total = rhs_ref[...] - own_ref[...]
    for ref in arrived:
        total -= ref[...].astype(F32)
    half = total.shape[1] // 2
    first = lax.rem(lax.axis_index("row"), 2) == 0
    kept = jnp.where(first, total[:, :half], total[:, half:])
    other = jnp.where(first, total[:, half:], total[:, :half])
    for k in range(0, len(taken), 2):
        kept -= taken[k][...]
        other -= taken[k + 1][...]
    kept_ref[...] = kept.astype(kept_ref.dtype)
    other_ref[...] = other.astype(other_ref.dtype)


def reduce_rows(rhs, target, own, arrived, taken, dtype):
    _, rows, width = rhs.shape
    taken = [part for pair in taken for part in pair]
    return pl.pallas_call(
        functools.partial(reduce_kernel, len(arrived)),
        grid=(1,),
        in_specs=[pl.BlockSpec((None, rows, width), lambda i: (target, 0, 0))]
        + [VMEM] * (1 + len(arrived) + len(taken)),
        out_specs=[VMEM, VMEM],
        out_shape=[jax.ShapeDtypeStruct((rows, width // 2), dtype)] * 2,
        compiler_params=params(8),
        cost_estimate=SMALL,
    )(rhs, own, *arrived, *taken)


def apply_kernel(index, parts, pairs, exact, full, own_ref, other_ref, *refs):
    shards, refs = refs[:parts], refs[parts:]
    held, outs = refs[: 2 * pairs], list(refs[2 * pairs :])
    me = lax.axis_index("row")
    core, chip = lax.rem(me, 2), me // 2
    rows = own_ref.shape[1]
    high, width = shards[0].shape
    low_ref = outs.pop()
    full_ref = outs.pop() if full else None
    total = jnp.zeros((high, width), F32)
    for mask, shard in enumerate(shards):
        cut = pl.ds(pl.multiple_of((chip ^ mask) * high, high), high)
        both = jnp.concatenate([own_ref[index, :, cut], other_ref[index, :, cut]], axis=0)
        total += jnp.dot(both, shard[...], preferred_element_type=F32)
        if full:
            full_ref[cut, :] = shard[...]
    for half, place in ((0, core), (1, 1 - core)):
        found = total[half * rows : (half + 1) * rows]
        if pairs:
            found = held[half][...] - found
        if exact:
            outs[half][...] = found
        there = pl.ds(pl.multiple_of(place * rows, rows), rows)
        low_ref[there, :] = found.astype(BF16)


def apply_rows(matrices, index, shards, held, exact, full):
    _, rows, depth = matrices[0].shape
    high, width = shards[0].shape
    operands = [*matrices, *shards, *held]
    shapes = [jax.ShapeDtypeStruct((rows, width), F32)] * (2 * exact)
    shapes += [jax.ShapeDtypeStruct((depth, width), BF16)] * full
    shapes.append(jax.ShapeDtypeStruct((high, width), BF16))
    return pl.pallas_call(
        functools.partial(apply_kernel, index, len(shards), len(held) // 2, exact, full),
        in_specs=[VMEM] * len(operands),
        out_specs=[VMEM] * len(shapes),
        out_shape=shapes,
        compiler_params=params(8),
        cost_estimate=SMALL,
    )(*operands)


def rows_kernel(places, matrix_ref, kept_ref, other_ref, *outs):
    for k, place in enumerate(places):
        for ref, out in zip((kept_ref, other_ref), outs[2 * k : 2 * k + 2]):
            out[...] = jnp.dot(matrix_ref[place], ref[...], preferred_element_type=F32)


def own_rows(matrices, places, kept, other):
    _, rows, _ = matrices.shape
    found = pl.pallas_call(
        functools.partial(rows_kernel, places),
        in_specs=[VMEM] * 3,
        out_specs=[VMEM] * (2 * len(places)),
        out_shape=[jax.ShapeDtypeStruct((rows, kept.shape[1]), F32)] * (2 * len(places)),
        compiler_params=params(8),
        cost_estimate=SMALL,
    )(matrices, kept, other)
    return [found[2 * k : 2 * k + 2] for k in range(len(places))]


def after(value, token):
    return lax.optimization_barrier((value, token))[0]


def local(rhs, l_panel, x_solved, diag_inv, l_inner, row_count, col_count):
    steps, rows, depth = l_panel.shape
    width = rhs.shape[2]
    total = x_solved.shape[1]
    chips = row_count // 2
    core = lax.axis_index("row") % 2
    pieces = 4
    shifts = sorted(range(1, col_count), key=lambda s: (abs(2 * s - col_count), s)) + [0]
    near = [inner_index(target, target - 1) for target in range(1, steps)]
    far = [inner_index(target, earlier) for target in range(2, steps) for earlier in range(target - 1)]
    chunk_shapes = [jax.ShapeDtypeStruct((rows, width), BF16 if s else F32) for s in shifts]

    def swap(value):
        return lax.ppermute(value, "row", [(i, i ^ 1) for i in range(row_count)])

    def gather(value):
        others = [
            lax.ppermute(value, "row", [(i, i ^ (2 * mask)) for i in range(row_count)])
            for mask in range(1, chips)
        ]
        return [value, *others]

    def send_chunks(chunks):
        return [
            lax.ppermute(chunk, "col", [(i, (i + s) % col_count) for i in range(col_count)])
            for s, chunk in zip(shifts[:-1], chunks)
        ]

    def by_core(kept, other, axis):
        return jnp.where(
            core == 0,
            jnp.concatenate([kept, other], axis=axis),
            jnp.concatenate([other, kept], axis=axis),
        )

    diag_other, inner_other = swap(diag_inv), swap(l_inner)
    first = pl.pallas_call(
        functools.partial(first_kernel, shifts, 8),
        in_specs=[HBM, HBM],
        out_specs=[VMEM] * col_count,
        out_shape=chunk_shapes,
        scratch_shapes=[
            pltpu.VMEM((8, rows, depth // 8), BF16),
            pltpu.VMEM((8, depth // 8, total), BF16),
            pltpu.VMEM((rows, total), F32),
            pltpu.SemaphoreType.DMA((8,)),
            pltpu.SemaphoreType.DMA((8,)),
        ],
        compiler_params=params(56),
        cost_estimate=work(rows, depth, total),
    )(l_panel, x_solved)
    chunks = [first]
    arrived = {0: send_chunks(first[:-1])}
    found = pl.pallas_call(
        functools.partial(second_kernel, shifts, pieces, 2),
        in_specs=[HBM, HBM],
        out_specs=[HBM] * ((steps - 1) * col_count),
        out_shape=chunk_shapes * (steps - 1),
        scratch_shapes=[
            pltpu.VMEM((pieces, rows * (steps - 1), depth // pieces), BF16),
            pltpu.VMEM((pieces, depth // pieces, total), BF16),
            pltpu.VMEM((rows * (steps - 1), total), F32),
            pltpu.VMEM((steps - 1, col_count - 1, rows, width), BF16),
            pltpu.VMEM((steps - 1, rows, width), F32),
            pltpu.SemaphoreType.DMA((pieces, steps - 1)),
            pltpu.SemaphoreType.DMA((pieces,)),
            pltpu.SemaphoreType.DMA((steps - 1, col_count)),
        ],
        compiler_params=params(56),
        cost_estimate=work(rows * (steps - 1), depth, total),
    )(l_panel, after(x_solved, first[0]))
    chunks += [found[i * col_count : (i + 1) * col_count] for i in range(steps - 1)]
    taken = {target: [] for target in range(steps)}

    def reduced(target, token, dtype):
        own = after(chunks[target][-1], token)
        kept, other = reduce_rows(rhs, target, own, arrived[target], taken[target], dtype)
        return kept, swap(other)

    resid_low = by_core(*reduced(0, found[0], BF16), 0)
    results = []
    for target in range(steps):
        last = target + 1 == steps
        shards = gather(resid_low)
        if target == 0:
            arrived[1] = send_chunks(after(chunks[1][:-1], resid_low))
            diag = load((after(diag_inv, resid_low), diag_other), range(steps))
        kept, other, solved_low = apply_rows(diag, target, shards, [], True, False)
        results.append((kept, other))
        if last:
            break
        shards = gather(solved_low)
        if target + 2 < steps:
            arrived[target + 2] = send_chunks(after(chunks[target + 2][:-1], solved_low))
        if target == 0:
            inner = load((after(l_inner, solved_low), inner_other), near)
        held = reduced(target + 1, solved_low, F32)
        *full, resid_low = apply_rows(inner, target, shards, held, False, target + 2 < steps)
        if full:
            followers = range(target + 2, steps)
            places = [far.index(inner_index(follower, target)) for follower in followers]
            whole = after(full[0], resid_low)
            if target == 0:
                (far_own,) = load((after(l_inner, resid_low),), far)
            for follower, pair in zip(followers, own_rows(far_own, places, whole, swap(whole))):
                taken[follower].append(pair)
    before = jnp.stack([other for _, other in results[:-1]])
    swapped = swap(after(before, resid_low))
    others = [swapped[k] for k in range(steps - 1)] + [swap(results[-1][1])]
    return jnp.stack([by_core(kept, other, 1) for (kept, _), other in zip(results, others)], axis=0)


def solution(mesh):
    in_specs = (
        P(None, "row", "col"),
        P(None, "row", "col"),
        P("col", None),
        P(None, "row", None),
        P(None, "row", None),
    )
    out_specs = P(None, "row", "col")
    body = functools.partial(local, row_count=mesh.shape["row"], col_count=mesh.shape["col"])
    return jax.shard_map(body, mesh=mesh, in_specs=in_specs, out_specs=out_specs, check_vma=False)
```

```python
import functools

import jax
import jax.numpy as jnp
from jax import lax
from jax.experimental import pallas as pl
from jax.experimental.pallas import tpu as pltpu
from jax.sharding import PartitionSpec as P

F32, BF16 = jnp.float32, jnp.bfloat16
VMEM = pl.BlockSpec(memory_space=pltpu.VMEM)
HBM = pl.BlockSpec(memory_space=pltpu.HBM)
SMALL = pl.CostEstimate(flops=1024, bytes_accessed=1024, transcendentals=0)


def inner_index(target, earlier):
    return target * (target - 1) // 2 + earlier


def params(mebibytes):
    return pltpu.CompilerParams(vmem_limit_bytes=mebibytes << 20)


def in_hbm(array):
    return pltpu.with_memory_space_constraint(array, pltpu.HBM)


def work(rows, depth, columns):
    return pl.CostEstimate(
        flops=2 * rows * depth * columns,
        bytes_accessed=2 * (rows + columns) * depth,
        transcendentals=0,
    )


def accumulate(total, piece, part, there=slice(None)):
    if piece == 0:
        total[:, there] = part
    else:
        total[:, there] += part


def first_kernel(shifts, pieces, l_ref, x_ref, *refs):
    count = len(shifts)
    outs, (l_buf, x_buf, total, l_sems, x_sems) = refs[:count], refs[count:]
    deep = x_ref.shape[0] // pieces
    width = x_ref.shape[1] // count
    mine = lax.axis_index("col")
    l_copies, x_copies = [], []
    for piece in range(pieces):
        cut = pl.ds(piece * deep, deep)
        l_copies.append(
            pltpu.make_async_copy(l_ref.at[0, :, cut], l_buf.at[piece], l_sems.at[piece])
        )
        x_copies.append(pltpu.make_async_copy(x_ref.at[cut], x_buf.at[piece], x_sems.at[piece]))
    for piece in range(pieces):
        l_copies[piece].start()
        x_copies[piece].start()
    for piece in range(pieces):
        l_copies[piece].wait()
        x_copies[piece].wait()
        accumulate(
            total, piece, jnp.dot(l_buf[piece], x_buf[piece], preferred_element_type=F32)
        )
    for shift, out in zip(shifts, outs):
        begin = pl.multiple_of(lax.rem(mine + shift, count) * width, width)
        out[...] = total[:, pl.ds(begin, width)].astype(out.dtype)


def later_kernel(shifts, pieces, flight, l_ref, x_ref, *refs):
    count = len(shifts)
    rows, depth = l_ref.shape[1:]
    blocks = l_ref.shape[0] - 1
    outs, refs = refs[: count + 2 * (blocks - 1)], refs[count + 2 * (blocks - 1) :]
    l_buf, x_buf, total, low, exact, l_sems, x_sems, out_sems = refs
    deep = depth // pieces
    width = x_ref.shape[1] // count
    mine = lax.axis_index("col")
    copies = []
    for piece in range(pieces):
        cut = pl.ds(piece * deep, deep)
        copies.append(
            [
                pltpu.make_async_copy(
                    l_ref.at[block + 1, :, cut],
                    l_buf.at[piece, pl.ds(block * rows, rows)],
                    l_sems.at[piece, block],
                )
                for block in range(blocks)
            ]
            + [pltpu.make_async_copy(x_ref.at[cut], x_buf.at[piece], x_sems.at[piece])]
        )
    for row in copies[:flight]:
        for copy in row:
            copy.start()
    for piece in range(pieces):
        for copy in copies[piece]:
            copy.wait()
        if piece + flight < pieces:
            for copy in copies[piece + flight]:
                copy.start()
        accumulate(
            total, piece, jnp.dot(l_buf[piece], x_buf[piece], preferred_element_type=F32)
        )
    copies = []

    def found(block, chunk):
        begin = pl.multiple_of(chunk * width, width)
        return total[block * rows : (block + 1) * rows, pl.ds(begin, width)]

    def send_out(held, out):
        copy = pltpu.make_async_copy(held, out, out_sems.at[len(copies)])
        copy.start()
        copies.append(copy)

    for k, shift in enumerate(shifts):
        held = low.at[0, k] if shift else exact.at[0, 0]
        held[...] = found(0, lax.rem(mine + shift, count)).astype(held.dtype)
        send_out(held, outs[k])
    for block in range(1, blocks):
        for slot in range(count):
            held = (low if slot % 2 else exact).at[block, slot // 2]
            held[...] = found(block, mine ^ slot).astype(held.dtype)
        place = count + 2 * (block - 1)
        send_out(low.at[block, pl.ds(0, count // 2)], outs[place])
        send_out(exact.at[block], outs[place + 1])
    for copy in copies:
        copy.wait()


def combine_kernel(exact_ref, arrived_ref, low_out, exact_out):
    for k in range(exact_ref.shape[0]):
        out = low_out if k % 2 else exact_out
        out[k // 2] = (exact_ref[k] + arrived_ref[k].astype(F32)).astype(out.dtype)


def combine(exact, arrived):
    count, rows, width = exact.shape
    return pl.pallas_call(
        combine_kernel,
        in_specs=[VMEM] * 2,
        out_specs=[VMEM] * 2,
        out_shape=[pltpu.VMEM((count // 2, rows, width), dtype) for dtype in (BF16, F32)],
        compiler_params=params(8),
        cost_estimate=SMALL,
    )(exact, arrived)


def load_kernel(stacks, *refs):
    count = len(stacks)
    ins, outs, sems = refs[:count], refs[count:-1], refs[-1]
    copies = [
        pltpu.make_async_copy(ins[k].at[index], outs[k].at[place], sems.at[k, place])
        for k, indices in enumerate(stacks)
        for place, index in enumerate(indices)
    ]
    for copy in copies:
        copy.start()
    for copy in copies:
        copy.wait()


def load(*stacks):
    picks = tuple(tuple(indices) for _, indices in stacks)
    return pl.pallas_call(
        functools.partial(load_kernel, picks),
        in_specs=[HBM] * len(stacks),
        out_specs=[VMEM] * len(stacks),
        out_shape=[
            pltpu.VMEM((len(indices), *array.shape[1:]), array.dtype) for array, indices in stacks
        ],
        scratch_shapes=[pltpu.SemaphoreType.DMA((len(stacks), max(map(len, picks))))],
        compiler_params=params(8),
        cost_estimate=SMALL,
    )(*[array for array, _ in stacks])


def reduce_kernel(parts, rhs_ref, own_ref, *refs):
    arrived, refs = refs[:parts], refs[parts:]
    taken, (kept_ref, other_ref) = refs[:-2], refs[-2:]
    total = rhs_ref[...] - own_ref[...].reshape(rhs_ref.shape)
    for ref in arrived:
        total -= ref[...].reshape(rhs_ref.shape).astype(F32)
    half = total.shape[1] // 2
    first = lax.rem(lax.axis_index("row"), 2) == 0
    kept = jnp.where(first, total[:, :half], total[:, half:])
    other = jnp.where(first, total[:, half:], total[:, :half])
    for k in range(0, len(taken), 2):
        kept -= taken[k][...]
        other -= taken[k + 1][...]
    kept_ref[...] = kept.astype(kept_ref.dtype)
    other_ref[...] = other.astype(other_ref.dtype)


def reduce_rows(rhs, target, own, arrived, taken, dtype):
    _, rows, width = rhs.shape
    taken = [part for pair in taken for part in pair]
    return pl.pallas_call(
        functools.partial(reduce_kernel, len(arrived)),
        grid=(1,),
        in_specs=[pl.BlockSpec((None, rows, width), lambda i: (target, 0, 0))]
        + [VMEM] * (1 + len(arrived) + len(taken)),
        out_specs=[VMEM, VMEM],
        out_shape=[jax.ShapeDtypeStruct((rows, width // 2), dtype)] * 2,
        compiler_params=params(8),
        cost_estimate=SMALL,
    )(rhs, own, *arrived, *taken)


def apply_kernel(index, parts, pairs, exact, full, low, own_ref, other_ref, *refs):
    shards, refs = refs[:parts], refs[parts:]
    held, outs = refs[: 2 * pairs], list(refs[2 * pairs :])
    me = lax.axis_index("row")
    core, chip = lax.rem(me, 2), me // 2
    rows = own_ref.shape[1]
    high, width = shards[0].shape
    low_ref = outs.pop() if low else None
    full_ref = outs.pop() if full else None
    total = jnp.zeros((high, width), F32)
    for mask, shard in enumerate(shards):
        cut = pl.ds(pl.multiple_of((chip ^ mask) * high, high), high)
        both = jnp.concatenate([own_ref[index, :, cut], other_ref[index, :, cut]], axis=0)
        total += jnp.dot(both, shard[...], preferred_element_type=F32)
        if full:
            full_ref[cut, :] = shard[...]
    for half, place in ((0, core), (1, 1 - core)):
        found = total[half * rows : (half + 1) * rows]
        if pairs:
            found = held[half][...] - found
        if exact:
            outs[half][...] = found
        if low:
            there = pl.ds(pl.multiple_of(place * rows, rows), rows)
            low_ref[there, :] = found.astype(BF16)


def apply_rows(matrices, index, shards, held, exact, full, low):
    _, rows, depth = matrices[0].shape
    high, width = shards[0].shape
    operands = [*matrices, *shards, *held]
    shapes = [pltpu.VMEM((rows, width), F32)] * (2 * exact)
    shapes += [pltpu.VMEM((depth, width), BF16)] * full
    shapes += [pltpu.VMEM((high, width), BF16)] * low
    return pl.pallas_call(
        functools.partial(apply_kernel, index, len(shards), len(held) // 2, exact, full, low),
        in_specs=[VMEM] * len(operands),
        out_specs=[VMEM] * len(shapes),
        out_shape=shapes,
        compiler_params=params(8),
        cost_estimate=SMALL,
    )(*operands)


def rows_kernel(places, matrix_ref, kept_ref, other_ref, *outs):
    for k, place in enumerate(places):
        for ref, out in zip((kept_ref, other_ref), outs[2 * k : 2 * k + 2]):
            out[...] = jnp.dot(matrix_ref[place], ref[...], preferred_element_type=F32)


def own_rows(matrices, places, kept, other):
    _, rows, _ = matrices.shape
    found = pl.pallas_call(
        functools.partial(rows_kernel, places),
        in_specs=[VMEM] * 3,
        out_specs=[VMEM] * (2 * len(places)),
        out_shape=[jax.ShapeDtypeStruct((rows, kept.shape[1]), F32)] * (2 * len(places)),
        compiler_params=params(8),
        cost_estimate=SMALL,
    )(matrices, kept, other)
    return [found[2 * k : 2 * k + 2] for k in range(len(places))]


def after(value, token):
    return lax.optimization_barrier((value, token))[0]


def local(rhs, l_panel, x_solved, diag_inv, l_inner, row_count, col_count):
    steps, rows, depth = l_panel.shape
    width = rhs.shape[2]
    total = x_solved.shape[1]
    chips = row_count // 2
    core = lax.axis_index("row") % 2
    pieces = 4
    shifts = sorted(range(1, col_count), key=lambda s: (abs(2 * s - col_count), s)) + [0]
    near = [inner_index(target, target - 1) for target in range(1, steps)]
    far = [inner_index(target, earlier) for target in range(2, steps) for earlier in range(target - 1)]
    chunk_shapes = [jax.ShapeDtypeStruct((rows, width), BF16 if s else F32) for s in shifts]

    def swap(value):
        return lax.ppermute(value, "row", [(i, i ^ 1) for i in range(row_count)])

    def gather(value, token=None):
        late = value if token is None else after(value, token)
        others = [
            lax.ppermute(
                late if mask == 1 else value, "row", [(i, i ^ (2 * mask)) for i in range(row_count)]
            )
            for mask in range(1, chips)
        ]
        return [value, *others]

    def by_core(kept, other, axis):
        return jnp.where(
            core == 0,
            jnp.concatenate([kept, other], axis=axis),
            jnp.concatenate([other, kept], axis=axis),
        )

    diag_other, inner_other = swap(diag_inv), swap(l_inner)
    first = pl.pallas_call(
        functools.partial(first_kernel, shifts, 8),
        in_specs=[HBM, HBM],
        out_specs=[VMEM] * col_count,
        out_shape=chunk_shapes,
        scratch_shapes=[
            pltpu.VMEM((8, rows, depth // 8), BF16),
            pltpu.VMEM((8, depth // 8, total), BF16),
            pltpu.VMEM((rows, total), F32),
            pltpu.SemaphoreType.DMA((8,)),
            pltpu.SemaphoreType.DMA((8,)),
        ],
        compiler_params=params(16),
        cost_estimate=work(rows, depth, total),
    )(in_hbm(l_panel), in_hbm(x_solved))
    chunks, arrived = {0: first}, {target: [] for target in range(steps)}

    def send(target, which, token):
        arrived[target] += [
            lax.ppermute(
                after(chunks[target][k], token),
                "col",
                [(i, (i + shifts[k]) % col_count) for i in range(col_count)],
            )
            for k in which
        ]

    ahead, behind = range(1), range(1, col_count - 1)
    send(0, range(col_count - 1), first[0])

    blocks = steps - 1
    shapes = list(chunk_shapes)
    for _ in range(blocks - 1):
        shapes += [jax.ShapeDtypeStruct((col_count // 2, rows, width), t) for t in (BF16, F32)]
    found = pl.pallas_call(
        functools.partial(later_kernel, shifts, pieces, 2),
        in_specs=[HBM] * 2,
        out_specs=[HBM] * len(shapes),
        out_shape=[pltpu.HBM(shape.shape, shape.dtype) for shape in shapes],
        scratch_shapes=[
            pltpu.VMEM((pieces, rows * blocks, depth // pieces), BF16),
            pltpu.VMEM((pieces, depth // pieces, total), BF16),
            pltpu.VMEM((rows * blocks, total), F32),
            pltpu.VMEM((blocks, col_count - 1, rows, width), BF16),
            pltpu.VMEM((blocks, col_count // 2, rows, width), F32),
            pltpu.SemaphoreType.DMA((pieces, blocks)),
            pltpu.SemaphoreType.DMA((pieces,)),
            pltpu.SemaphoreType.DMA((len(shapes),)),
        ],
        compiler_params=params(60),
        cost_estimate=work(rows * blocks, depth, total),
    )(in_hbm(l_panel), in_hbm(after(x_solved, first[0])))
    chunks[1], found = found[:col_count], found[col_count:]
    halves = {target: found[2 * target - 4 : 2 * target - 2] for target in range(2, steps)}

    def halve(target, stage, token):
        low, exact = halves[target]
        if stage:
            arrived_low = arrived[target]
            low, exact = combine(after(exact, token), arrived_low)
        else:
            low = after(low, token)
        pairs = [(i, i ^ (1 << stage)) for i in range(col_count)]
        halves[target] = (low, exact)
        arrived[target] = lax.ppermute(low, "col", pairs)

    taken = {target: [] for target in range(steps)}

    def reduced(target, token, dtype):
        if target in chunks:
            own, parts = chunks[target][-1], arrived[target]
        else:
            own, parts = halves[target][1], [arrived[target]]
        return reduce_rows(rhs, target, after(own, token), parts, taken[target], dtype)

    kept, other = reduced(0, (chunks[1][0], diag_other), BF16)
    send(1, ahead, other)
    resid_low = by_core(kept, swap(other), 0)
    results, wholes = [], {}
    stages = (col_count - 1).bit_length()
    for target in range(steps):
        last = target + 1 == steps
        shards = gather(resid_low)
        if target == 0:
            later = in_hbm(after(diag_inv, resid_low))
            diag = {0: load((later, [0]), (in_hbm(diag_other), [0]))}
            send(1, behind, (resid_low, inner_other, diag[0]))
        elif not last:
            for stage in range(1, stages):
                halve(target + 1, stage, resid_low)
        else:
            before = jnp.stack([other for _, other in results])
            swapped = swap(after(before, resid_low))
            parts = [by_core(kept, swapped[k], 1) for k, (kept, _) in enumerate(results)]
            solved = jnp.stack([*parts, jnp.zeros_like(parts[0])])
            shards, solved = lax.optimization_barrier((shards, solved))
        kept, other, *low = apply_rows(diag[target], 0, shards, [], True, False, not last)
        results.append((kept, other))
        if last:
            break
        (solved_low,) = low
        shards = gather(solved_low, arrived[1][0] if target == 0 else None)
        if target == 0:
            inner = load((in_hbm(after(l_inner, solved_low)), near), (in_hbm(inner_other), near))
            token = (solved_low, inner)
        elif target == 1:
            (far_own,) = load((in_hbm(after(l_inner, solved_low)), far))
            token = solved_low
        else:
            token = solved_low
        if target + 2 < steps:
            halve(target + 2, 0, token)
        for earlier in list(wholes):
            followers = range(earlier + 2, steps)
            places = [far.index(inner_index(follower, earlier)) for follower in followers]
            for follower, pair in zip(followers, own_rows(far_own, places, *wholes.pop(earlier))):
                taken[follower].append(pair)
        kept, other = reduced(target + 1, token, F32)
        later = in_hbm(after(diag_inv, other))
        diag[target + 1] = load((later, [target + 1]), (in_hbm(diag_other), [target + 1]))
        held = (kept, swap(other))
        shards, diag[target + 1] = lax.optimization_barrier((shards, diag[target + 1]))
        *full, resid_low = apply_rows(inner, target, shards, held, False, target + 2 < steps, True)
        if full:
            whole = after(full[0], resid_low)
            wholes[target] = (whole, swap(whole))
    kept, other = results[-1]
    return lax.dynamic_update_slice(solved, by_core(kept, swap(other), 1)[None], (steps - 1, 0, 0))


def solution(mesh):
    in_specs = (
        P(None, "row", "col"),
        P(None, "row", "col"),
        P("col", None),
        P(None, "row", None),
        P(None, "row", None),
    )
    out_specs = P(None, "row", "col")
    body = functools.partial(local, row_count=mesh.shape["row"], col_count=mesh.shape["col"])
    return jax.shard_map(body, mesh=mesh, in_specs=in_specs, out_specs=out_specs, check_vma=False)
```

```python
import functools

import jax
import jax.numpy as jnp
from jax import lax
from jax.experimental import pallas as pl
from jax.experimental.pallas import tpu as pltpu
from jax.sharding import PartitionSpec as P

F32, BF16 = jnp.float32, jnp.bfloat16
VMEM = pl.BlockSpec(memory_space=pltpu.VMEM)
HBM = pl.BlockSpec(memory_space=pltpu.HBM)
SMALL = pl.CostEstimate(flops=1024, bytes_accessed=1024, transcendentals=0)


def inner_index(target, earlier):
    return target * (target - 1) // 2 + earlier


def params(mebibytes):
    return pltpu.CompilerParams(vmem_limit_bytes=mebibytes << 20)


def in_hbm(array):
    return pltpu.with_memory_space_constraint(array, pltpu.HBM)


def work(rows, depth, columns):
    return pl.CostEstimate(
        flops=2 * rows * depth * columns,
        bytes_accessed=2 * (rows + columns) * depth,
        transcendentals=0,
    )


def accumulate(total, piece, part, there=slice(None)):
    if piece == 0:
        total[:, there] = part
    else:
        total[:, there] += part


def first_kernel(shifts, pieces, l_ref, x_ref, *refs):
    count = len(shifts)
    outs, (l_buf, x_buf, total, l_sems, x_sems) = refs[:count], refs[count:]
    deep = x_ref.shape[0] // pieces
    width = x_ref.shape[1] // count
    mine = lax.axis_index("col")
    l_copies, x_copies = [], []
    for piece in range(pieces):
        cut = pl.ds(piece * deep, deep)
        l_copies.append(
            pltpu.make_async_copy(l_ref.at[0, :, cut], l_buf.at[piece], l_sems.at[piece])
        )
        x_copies.append(pltpu.make_async_copy(x_ref.at[cut], x_buf.at[piece], x_sems.at[piece]))
    for piece in range(pieces):
        l_copies[piece].start()
        x_copies[piece].start()
    for piece in range(pieces):
        l_copies[piece].wait()
        x_copies[piece].wait()
        accumulate(
            total, piece, jnp.dot(l_buf[piece], x_buf[piece], preferred_element_type=F32)
        )
    for shift, out in zip(shifts, outs):
        begin = pl.multiple_of(lax.rem(mine + shift, count) * width, width)
        out[...] = total[:, pl.ds(begin, width)].astype(out.dtype)


def later_kernel(count, pieces, flight, l_ref, x_ref, *refs):
    rows, depth = l_ref.shape[1:]
    blocks = l_ref.shape[0] - 1
    outs, refs = refs[: 2 * blocks], refs[2 * blocks :]
    l_buf, x_buf, total, low, exact, l_sems, x_sems, out_sems = refs
    deep = depth // pieces
    width = x_ref.shape[1] // count
    mine = lax.axis_index("col")
    copies = []
    for piece in range(pieces):
        cut = pl.ds(piece * deep, deep)
        copies.append(
            [
                pltpu.make_async_copy(
                    l_ref.at[block + 1, :, cut],
                    l_buf.at[piece, pl.ds(block * rows, rows)],
                    l_sems.at[piece, block],
                )
                for block in range(blocks)
            ]
            + [pltpu.make_async_copy(x_ref.at[cut], x_buf.at[piece], x_sems.at[piece])]
        )
    for row in copies[:flight]:
        for copy in row:
            copy.start()
    for piece in range(pieces):
        for copy in copies[piece]:
            copy.wait()
        if piece + flight < pieces:
            for copy in copies[piece + flight]:
                copy.start()
        accumulate(
            total, piece, jnp.dot(l_buf[piece], x_buf[piece], preferred_element_type=F32)
        )
    copies = []

    def found(block, chunk):
        begin = pl.multiple_of(chunk * width, width)
        return total[block * rows : (block + 1) * rows, pl.ds(begin, width)]

    def send_out(held, out):
        copy = pltpu.make_async_copy(held, out, out_sems.at[len(copies)])
        copy.start()
        copies.append(copy)

    for block in range(blocks):
        for slot in range(count):
            held = (low if slot % 2 else exact).at[block, slot // 2]
            held[...] = found(block, mine ^ slot).astype(held.dtype)
        send_out(low.at[block], outs[2 * block])
        send_out(exact.at[block], outs[2 * block + 1])
    for copy in copies:
        copy.wait()


def combine_kernel(exact_ref, arrived_ref, low_out, exact_out):
    for k in range(exact_ref.shape[0]):
        out = low_out if k % 2 else exact_out
        out[k // 2] = (exact_ref[k] + arrived_ref[k].astype(F32)).astype(out.dtype)


def combine(exact, arrived):
    count, rows, width = exact.shape
    return pl.pallas_call(
        combine_kernel,
        in_specs=[VMEM] * 2,
        out_specs=[VMEM] * 2,
        out_shape=[pltpu.VMEM((count // 2, rows, width), dtype) for dtype in (BF16, F32)],
        compiler_params=params(8),
        cost_estimate=SMALL,
    )(exact, arrived)


def load_kernel(indices, *refs):
    count = len(indices)
    ins, outs, sems = refs[:count], refs[count:-1], refs[-1]
    copies = [
        pltpu.make_async_copy(ref.at[index], out, sems.at[k])
        for k, (ref, out, index) in enumerate(zip(ins, outs, indices))
    ]
    for copy in copies:
        copy.start()
    for copy in copies:
        copy.wait()


def load(token, *picks):
    indices = tuple(index for _, _, index in picks for _ in range(2))
    arrays = [in_hbm(array) for own, other, _ in picks for array in (after(own, token), other)]
    found = pl.pallas_call(
        functools.partial(load_kernel, indices),
        in_specs=[HBM] * len(arrays),
        out_specs=[VMEM] * len(arrays),
        out_shape=[pltpu.VMEM(array.shape[1:], array.dtype) for array in arrays],
        scratch_shapes=[pltpu.SemaphoreType.DMA((len(arrays),))],
        compiler_params=params(8),
        cost_estimate=SMALL,
    )(*arrays)
    return [tuple(found[2 * k : 2 * k + 2]) for k in range(len(picks))]


def reduce_kernel(rhs_ref, own_ref, *refs):
    arrived, (kept_ref, other_ref) = refs[:-2], refs[-2:]
    total = rhs_ref[...] - own_ref[...].reshape(rhs_ref.shape)
    for ref in arrived:
        total -= ref[...].reshape(rhs_ref.shape).astype(F32)
    half = total.shape[1] // 2
    first = lax.rem(lax.axis_index("row"), 2) == 0
    kept_ref[...] = jnp.where(first, total[:, :half], total[:, half:]).astype(kept_ref.dtype)
    other_ref[...] = jnp.where(first, total[:, half:], total[:, :half]).astype(other_ref.dtype)


def reduce_rows(rhs, target, own, arrived, dtype):
    _, rows, width = rhs.shape
    return pl.pallas_call(
        reduce_kernel,
        grid=(1,),
        in_specs=[pl.BlockSpec((None, rows, width), lambda i: (target, 0, 0))]
        + [VMEM] * (1 + len(arrived)),
        out_specs=[VMEM, VMEM],
        out_shape=[jax.ShapeDtypeStruct((rows, width // 2), dtype)] * 2,
        compiler_params=params(8),
        cost_estimate=SMALL,
    )(rhs, own, *arrived)


def apply_kernel(masks, pairs, sign, exact, low, own_ref, other_ref, *refs):
    shards, refs = refs[: len(masks)], refs[len(masks) :]
    held, outs = refs[: 2 * pairs], refs[2 * pairs :]
    me = lax.axis_index("row")
    core, chip = lax.rem(me, 2), me // 2
    rows = own_ref.shape[0]
    high, width = shards[0].shape
    total = jnp.zeros((high, width), F32)
    for mask, shard in zip(masks, shards):
        cut = pl.ds(pl.multiple_of((chip ^ mask) * high, high), high)
        both = jnp.concatenate([own_ref[:, cut], other_ref[:, cut]], axis=0)
        total += jnp.dot(both, shard[...], preferred_element_type=F32)
    for half, place in ((0, core), (1, 1 - core)):
        found = total[half * rows : (half + 1) * rows]
        if pairs:
            base = held[half][...]
            for pair in range(1, pairs):
                base -= held[2 * pair + half][...]
            found = base + found if sign > 0 else base - found
        if exact:
            outs[half][...] = found
        if low:
            there = pl.ds(pl.multiple_of(place * rows, rows), rows)
            outs[-1][there, :] = found.astype(BF16)


def apply_rows(matrix, shards, held, sign, exact, low):
    masks = tuple(shards)
    rows = matrix[0].shape[0]
    high, width = shards[masks[0]].shape
    operands = [*matrix, *shards.values(), *(part for pair in held for part in pair)]
    shapes = [pltpu.VMEM((rows, width), F32)] * (2 * exact)
    shapes += [pltpu.VMEM((high, width), BF16)] * low
    return pl.pallas_call(
        functools.partial(apply_kernel, masks, len(held), sign, exact, low),
        in_specs=[VMEM] * len(operands),
        out_specs=[VMEM] * len(shapes),
        out_shape=shapes,
        compiler_params=params(8),
        cost_estimate=SMALL,
    )(*operands)


def rows_kernel(masks, matrix_ref, *refs):
    shards, out_ref = refs[:-1], refs[-1]
    chip = lax.axis_index("row") // 2
    high, width = shards[0].shape
    total = jnp.zeros(out_ref.shape, F32)
    for mask, shard in zip(masks, shards):
        cut = pl.ds(pl.multiple_of((chip ^ mask) * high, high), high)
        total += jnp.dot(matrix_ref[:, cut], shard[...], preferred_element_type=F32)
    out_ref[...] = total


def last_rows(matrix, shards):
    masks = tuple(shards)

    def rows_of(part):
        shape = (part.shape[0], shards[0].shape[1])
        return pl.pallas_call(
            functools.partial(rows_kernel, masks),
            in_specs=[VMEM] * (1 + len(masks)),
            out_specs=VMEM,
            out_shape=pltpu.VMEM(shape, F32),
            compiler_params=params(8),
            cost_estimate=SMALL,
        )(part, *shards.values())

    other = rows_of(matrix[1])
    return rows_of(after(matrix[0], other)), other


def after(value, token):
    return lax.optimization_barrier((value, token))[0]


def local(rhs, l_panel, x_solved, diag_inv, l_inner, row_count, col_count):
    steps, rows, depth = l_panel.shape
    width = rhs.shape[2]
    total = x_solved.shape[1]
    chips = row_count // 2
    core = lax.axis_index("row") % 2
    pieces = 4
    shifts = sorted(range(1, col_count), key=lambda s: (abs(2 * s - col_count), s)) + [0]
    chunk_shapes = [jax.ShapeDtypeStruct((rows, width), BF16 if s else F32) for s in shifts]

    def swap(value):
        return lax.ppermute(value, "row", [(i, i ^ 1) for i in range(row_count)])

    def gather(value, token=None):
        late = value if token is None else after(value, token)
        shards = {0: value}
        for mask in range(1, chips):
            pairs = [(i, i ^ (2 * mask)) for i in range(row_count)]
            shards[mask] = lax.ppermute(late if mask == 1 else value, "row", pairs)
        return shards

    def by_core(kept, other, axis):
        return jnp.where(
            core == 0,
            jnp.concatenate([kept, other], axis=axis),
            jnp.concatenate([other, kept], axis=axis),
        )

    diag_other, inner_other = swap(diag_inv), swap(l_inner)
    first = pl.pallas_call(
        functools.partial(first_kernel, shifts, 8),
        in_specs=[HBM, HBM],
        out_specs=[VMEM] * col_count,
        out_shape=chunk_shapes,
        scratch_shapes=[
            pltpu.VMEM((8, rows, depth // 8), BF16),
            pltpu.VMEM((8, depth // 8, total), BF16),
            pltpu.VMEM((rows, total), F32),
            pltpu.SemaphoreType.DMA((8,)),
            pltpu.SemaphoreType.DMA((8,)),
        ],
        compiler_params=params(16),
        cost_estimate=work(rows, depth, total),
    )(in_hbm(l_panel), in_hbm(x_solved))
    chunks, arrived = {0: first}, {target: [] for target in range(steps)}

    def send(target, which, token):
        arrived[target] += [
            lax.ppermute(
                after(chunks[target][k], token),
                "col",
                [(i, (i + shifts[k]) % col_count) for i in range(col_count)],
            )
            for k in which
        ]

    send(0, [*range(1, col_count - 1), 0], first[0])

    blocks = steps - 1
    shapes = []
    for _ in range(blocks):
        shapes += [jax.ShapeDtypeStruct((col_count // 2, rows, width), t) for t in (BF16, F32)]
    found = pl.pallas_call(
        functools.partial(later_kernel, col_count, pieces, 2),
        in_specs=[HBM] * 2,
        out_specs=[HBM] * len(shapes),
        out_shape=[pltpu.HBM(shape.shape, shape.dtype) for shape in shapes],
        scratch_shapes=[
            pltpu.VMEM((pieces, rows * blocks, depth // pieces), BF16),
            pltpu.VMEM((pieces, depth // pieces, total), BF16),
            pltpu.VMEM((rows * blocks, total), F32),
            pltpu.VMEM((blocks, col_count // 2, rows, width), BF16),
            pltpu.VMEM((blocks, col_count // 2, rows, width), F32),
            pltpu.SemaphoreType.DMA((pieces, blocks)),
            pltpu.SemaphoreType.DMA((pieces,)),
            pltpu.SemaphoreType.DMA((len(shapes),)),
        ],
        compiler_params=params(60),
        cost_estimate=work(rows * blocks, depth, total),
    )(in_hbm(l_panel), in_hbm(after(x_solved, first[0])))
    halves = {target: found[2 * target - 2 : 2 * target] for target in range(1, steps)}

    def halve(target, stage, token):
        low, exact = halves[target]
        if stage:
            arrived_low = arrived[target]
            low, exact = combine(after(exact, token), arrived_low)
        else:
            low = after(low, token)
        pairs = [(i, i ^ (1 << stage)) for i in range(col_count)]
        halves[target] = (low, exact)
        arrived[target] = lax.ppermute(low, "col", pairs)


    def reduced(target, token, dtype):
        if target in chunks:
            own, parts = chunks[target][-1], arrived[target]
        else:
            own, parts = halves[target][1], [arrived[target]]
        return reduce_rows(rhs, target, after(own, token), parts, dtype)

    kept, other = reduced(0, (found[0], diag_other), BF16)
    halve(1, 0, other)
    resid_low = by_core(kept, swap(other), 0)
    results, solved_shards = [], {}
    products = {target: [] for target in range(steps)}
    stages = (col_count - 1).bit_length()
    diag_pick = [(diag_inv, diag_other, target) for target in range(steps)]
    inner_pick = [(l_inner, inner_other, index) for index in range(l_inner.shape[0])]
    near_matrix = {}
    for target in range(steps):
        last = target + 1 == steps
        shards = gather(resid_low)
        if target == 0:
            diag_matrix, near_matrix[0] = load(resid_low, diag_pick[0], inner_pick[0])
            for stage in range(1, stages):
                halve(1, stage, diag_matrix)
        elif not last:
            diag_matrix, near_matrix[target] = load(
                resid_low, diag_pick[target], inner_pick[inner_index(target + 1, target)]
            )
            if target > 1:
                halve(target + 1, 0, resid_low)
            for stage in range(1, stages):
                halve(target + 1, stage, (resid_low, diag_matrix))
        else:
            (diag_matrix,) = load(resid_low, diag_pick[target])
            before = jnp.stack([other for _, other in results])
            swapped = swap(after(before, resid_low))
            parts = [by_core(kept, swapped[k], 1) for k, (kept, _) in enumerate(results)]
            solved = jnp.stack([*parts, jnp.zeros_like(parts[0])])
            shards[0], solved, diag_matrix = lax.optimization_barrier((shards[0], solved, diag_matrix))
        if last:
            kept, other = last_rows(diag_matrix, shards)
        else:
            kept, other, *low = apply_rows(diag_matrix, shards, [], 1, True, True)
        results.append((kept, other))
        if last:
            break
        (solved_low,) = low
        shards = gather(solved_low)
        solved_shards[target] = shards
        token = solved_low
        if target == 0:
            pass
        if target == 0:
            halve(target + 2, 0, token)
        kept, other = reduced(target + 1, token, F32)
        held = [(kept, swap(other))]
        if target:
            earlier = range(target)
            loaded = load(solved_low, *[inner_pick[inner_index(target + 1, k)] for k in earlier])
            for k, matrix in zip(earlier, loaded):
                held.append(apply_rows(matrix, solved_shards[k], [], 1, True, False))
        (resid_low,) = apply_rows(near_matrix[target], shards, held, -1, False, True)
    kept, other = results[-1]
    return lax.dynamic_update_slice(solved, by_core(kept, swap(other), 1)[None], (steps - 1, 0, 0))


def solution(mesh):
    in_specs = (
        P(None, "row", "col"),
        P(None, "row", "col"),
        P("col", None),
        P(None, "row", None),
        P(None, "row", None),
    )
    out_specs = P(None, "row", "col")
    body = functools.partial(local, row_count=mesh.shape["row"], col_count=mesh.shape["col"])
    return jax.shard_map(body, mesh=mesh, in_specs=in_specs, out_specs=out_specs, check_vma=False)
```

```python
import functools

import jax
import jax.numpy as jnp
from jax import lax
from jax.experimental import pallas as pl
from jax.experimental.pallas import tpu as pltpu
from jax.sharding import PartitionSpec as P

F32, BF16 = jnp.float32, jnp.bfloat16
VMEM = pl.BlockSpec(memory_space=pltpu.VMEM)
HBM = pl.BlockSpec(memory_space=pltpu.HBM)
SMALL = pl.CostEstimate(flops=1024, bytes_accessed=1024, transcendentals=0)


def inner_index(target, earlier):
    return target * (target - 1) // 2 + earlier


def params(mebibytes):
    return pltpu.CompilerParams(vmem_limit_bytes=mebibytes << 20)


def in_hbm(array):
    return pltpu.with_memory_space_constraint(array, pltpu.HBM)


def work(rows, depth, columns):
    return pl.CostEstimate(
        flops=2 * rows * depth * columns,
        bytes_accessed=2 * (rows + columns) * depth,
        transcendentals=0,
    )


def accumulate(total, piece, part, there=slice(None)):
    if piece == 0:
        total[:, there] = part
    else:
        total[:, there] += part


def first_kernel(shifts, pieces, l_ref, x_ref, *refs):
    count = len(shifts)
    outs, (l_buf, x_buf, total, l_sems, x_sems) = refs[:count], refs[count:]
    deep = x_ref.shape[0] // pieces
    width = x_ref.shape[1] // count
    mine = lax.axis_index("col")
    l_copies, x_copies = [], []
    for piece in range(pieces):
        cut = pl.ds(piece * deep, deep)
        l_copies.append(
            pltpu.make_async_copy(l_ref.at[0, :, cut], l_buf.at[piece], l_sems.at[piece])
        )
        x_copies.append(pltpu.make_async_copy(x_ref.at[cut], x_buf.at[piece], x_sems.at[piece]))
    for piece in range(pieces):
        l_copies[piece].start()
        x_copies[piece].start()
    for piece in range(pieces):
        l_copies[piece].wait()
        x_copies[piece].wait()
        accumulate(
            total, piece, jnp.dot(l_buf[piece], x_buf[piece], preferred_element_type=F32)
        )
    for shift, out in zip(shifts, outs):
        begin = pl.multiple_of(lax.rem(mine + shift, count) * width, width)
        out[...] = total[:, pl.ds(begin, width)].astype(out.dtype)


def later_kernel(count, pieces, flight, l_ref, x_ref, *refs):
    rows, depth = l_ref.shape[1:]
    blocks = l_ref.shape[0] - 1
    outs, refs = refs[: 2 * blocks], refs[2 * blocks :]
    l_buf, x_buf, total, low, exact, l_sems, x_sems, out_sems = refs
    deep = depth // pieces
    width = x_ref.shape[1] // count
    mine = lax.axis_index("col")
    copies = []
    for piece in range(pieces):
        cut = pl.ds(piece * deep, deep)
        copies.append(
            [
                pltpu.make_async_copy(
                    l_ref.at[block + 1, :, cut],
                    l_buf.at[piece, pl.ds(block * rows, rows)],
                    l_sems.at[piece, block],
                )
                for block in range(blocks)
            ]
            + [pltpu.make_async_copy(x_ref.at[cut], x_buf.at[piece], x_sems.at[piece])]
        )
    for row in copies[:flight]:
        for copy in row:
            copy.start()
    for piece in range(pieces):
        for copy in copies[piece]:
            copy.wait()
        if piece + flight < pieces:
            for copy in copies[piece + flight]:
                copy.start()
        accumulate(
            total, piece, jnp.dot(l_buf[piece], x_buf[piece], preferred_element_type=F32)
        )
    copies = []

    def found(block, chunk):
        begin = pl.multiple_of(chunk * width, width)
        return total[block * rows : (block + 1) * rows, pl.ds(begin, width)]

    def send_out(held, out):
        copy = pltpu.make_async_copy(held, out, out_sems.at[len(copies)])
        copy.start()
        copies.append(copy)

    for block in range(blocks):
        for slot in range(count):
            held = (low if slot % 2 else exact).at[block, slot // 2]
            held[...] = found(block, mine ^ slot).astype(held.dtype)
        send_out(low.at[block], outs[2 * block])
        send_out(exact.at[block], outs[2 * block + 1])
    for copy in copies:
        copy.wait()


def combine_kernel(exact_ref, arrived_ref, low_out, exact_out):
    for k in range(exact_ref.shape[0]):
        out = low_out if k % 2 else exact_out
        out[k // 2] = (exact_ref[k] + arrived_ref[k].astype(F32)).astype(out.dtype)


def combine(exact, arrived):
    count, rows, width = exact.shape
    return pl.pallas_call(
        combine_kernel,
        in_specs=[VMEM] * 2,
        out_specs=[VMEM] * 2,
        out_shape=[pltpu.VMEM((count // 2, rows, width), dtype) for dtype in (BF16, F32)],
        compiler_params=params(8),
        cost_estimate=SMALL,
    )(exact, arrived)


def load_kernel(indices, *refs):
    count = len(indices)
    ins, outs, sems = refs[:count], refs[count:-1], refs[-1]
    copies = [
        pltpu.make_async_copy(ref.at[index], out, sems.at[k])
        for k, (ref, out, index) in enumerate(zip(ins, outs, indices))
    ]
    for copy in copies:
        copy.start()
    for copy in copies:
        copy.wait()


def load(token, *picks):
    indices = tuple(index for _, _, index in picks for _ in range(2))
    arrays = [in_hbm(array) for own, other, _ in picks for array in (after(own, token), other)]
    found = pl.pallas_call(
        functools.partial(load_kernel, indices),
        in_specs=[HBM] * len(arrays),
        out_specs=[VMEM] * len(arrays),
        out_shape=[pltpu.VMEM(array.shape[1:], array.dtype) for array in arrays],
        scratch_shapes=[pltpu.SemaphoreType.DMA((len(arrays),))],
        compiler_params=params(8),
        cost_estimate=SMALL,
    )(*arrays)
    return [tuple(found[2 * k : 2 * k + 2]) for k in range(len(picks))]


def reduce_kernel(rhs_ref, own_ref, *refs):
    arrived, (kept_ref, other_ref) = refs[:-2], refs[-2:]
    total = rhs_ref[...] - own_ref[...].reshape(rhs_ref.shape)
    for ref in arrived:
        total -= ref[...].reshape(rhs_ref.shape).astype(F32)
    half = total.shape[1] // 2
    first = lax.rem(lax.axis_index("row"), 2) == 0
    kept_ref[...] = jnp.where(first, total[:, :half], total[:, half:]).astype(kept_ref.dtype)
    other_ref[...] = jnp.where(first, total[:, half:], total[:, :half]).astype(other_ref.dtype)


def reduce_rows(rhs, target, own, arrived, dtype):
    _, rows, width = rhs.shape
    return pl.pallas_call(
        reduce_kernel,
        grid=(1,),
        in_specs=[pl.BlockSpec((None, rows, width), lambda i: (target, 0, 0))]
        + [VMEM] * (1 + len(arrived)),
        out_specs=[VMEM, VMEM],
        out_shape=[jax.ShapeDtypeStruct((rows, width // 2), dtype)] * 2,
        compiler_params=params(8),
        cost_estimate=SMALL,
    )(rhs, own, *arrived)


def apply_kernel(masks, pairs, sign, exact, low, own_ref, other_ref, *refs):
    shards, refs = refs[: len(masks)], refs[len(masks) :]
    held, outs = refs[: 2 * pairs], refs[2 * pairs :]
    me = lax.axis_index("row")
    core, chip = lax.rem(me, 2), me // 2
    rows = own_ref.shape[0]
    high, width = shards[0].shape
    total = jnp.zeros((high, width), F32)
    for mask, shard in zip(masks, shards):
        cut = pl.ds(pl.multiple_of((chip ^ mask) * high, high), high)
        both = jnp.concatenate([own_ref[:, cut], other_ref[:, cut]], axis=0)
        total += jnp.dot(both, shard[...], preferred_element_type=F32)
    for half, place in ((0, core), (1, 1 - core)):
        found = total[half * rows : (half + 1) * rows]
        if pairs:
            base = held[half][...]
            for pair in range(1, pairs):
                base -= held[2 * pair + half][...]
            found = base + found if sign > 0 else base - found
        if exact:
            outs[half][...] = found
        if low:
            there = pl.ds(pl.multiple_of(place * rows, rows), rows)
            outs[-1][there, :] = found.astype(BF16)


def apply_rows(matrix, shards, held, sign, exact, low):
    masks = tuple(shards)
    rows = matrix[0].shape[0]
    high, width = shards[masks[0]].shape
    operands = [*matrix, *shards.values(), *(part for pair in held for part in pair)]
    shapes = [pltpu.VMEM((rows, width), F32)] * (2 * exact)
    shapes += [pltpu.VMEM((high, width), BF16)] * low
    return pl.pallas_call(
        functools.partial(apply_kernel, masks, len(held), sign, exact, low),
        in_specs=[VMEM] * len(operands),
        out_specs=[VMEM] * len(shapes),
        out_shape=shapes,
        compiler_params=params(8),
        cost_estimate=SMALL,
    )(*operands)


def rows_kernel(masks, matrix_ref, *refs):
    shards, out_ref = refs[:-1], refs[-1]
    chip = lax.axis_index("row") // 2
    high, width = shards[0].shape
    total = jnp.zeros(out_ref.shape, F32)
    for mask, shard in zip(masks, shards):
        cut = pl.ds(pl.multiple_of((chip ^ mask) * high, high), high)
        total += jnp.dot(matrix_ref[:, cut], shard[...], preferred_element_type=F32)
    out_ref[...] = total


def last_rows(matrix, shards):
    masks = tuple(shards)

    def rows_of(part):
        shape = (part.shape[0], shards[0].shape[1])
        return pl.pallas_call(
            functools.partial(rows_kernel, masks),
            in_specs=[VMEM] * (1 + len(masks)),
            out_specs=VMEM,
            out_shape=pltpu.VMEM(shape, F32),
            compiler_params=params(8),
            cost_estimate=SMALL,
        )(part, *shards.values())

    other = rows_of(matrix[1])
    return rows_of(after(matrix[0], other)), other


def after(value, token):
    return lax.optimization_barrier((value, token))[0]


def local(rhs, l_panel, x_solved, diag_inv, l_inner, row_count, col_count):
    steps, rows, depth = l_panel.shape
    width = rhs.shape[2]
    total = x_solved.shape[1]
    chips = row_count // 2
    core = lax.axis_index("row") % 2
    pieces = 4
    shifts = sorted(range(1, col_count), key=lambda s: (abs(2 * s - col_count), s)) + [0]
    chunk_shapes = [jax.ShapeDtypeStruct((rows, width), BF16 if s else F32) for s in shifts]

    def swap(value):
        return lax.ppermute(value, "row", [(i, i ^ 1) for i in range(row_count)])

    def gather(value, token=None, lower=False):
        late = value if token is None else after(value, token)
        shards = {0: value}
        for mask in range(1, chips):
            pairs = [(i, i ^ (2 * mask)) for i in range(row_count)]
            if lower and mask == chips - 1:
                pairs = [(i, j) for i, j in pairs if i < j]
            shards[mask] = lax.ppermute(late if mask == 1 else value, "row", pairs)
        return shards

    def by_core(kept, other, axis):
        return jnp.where(
            core == 0,
            jnp.concatenate([kept, other], axis=axis),
            jnp.concatenate([other, kept], axis=axis),
        )

    diag_other, inner_other = swap(diag_inv), swap(l_inner)
    first = pl.pallas_call(
        functools.partial(first_kernel, shifts, 8),
        in_specs=[HBM, HBM],
        out_specs=[VMEM] * col_count,
        out_shape=chunk_shapes,
        scratch_shapes=[
            pltpu.VMEM((8, rows, depth // 8), BF16),
            pltpu.VMEM((8, depth // 8, total), BF16),
            pltpu.VMEM((rows, total), F32),
            pltpu.SemaphoreType.DMA((8,)),
            pltpu.SemaphoreType.DMA((8,)),
        ],
        compiler_params=params(16),
        cost_estimate=work(rows, depth, total),
    )(in_hbm(l_panel), in_hbm(x_solved))
    chunks, arrived = {0: first}, {target: [] for target in range(steps)}

    def send(target, which, token):
        arrived[target] += [
            lax.ppermute(
                after(chunks[target][k], token),
                "col",
                [(i, (i + shifts[k]) % col_count) for i in range(col_count)],
            )
            for k in which
        ]

    send(0, [*range(1, col_count - 1), 0], first[0])

    blocks = steps - 1
    shapes = []
    for _ in range(blocks):
        shapes += [jax.ShapeDtypeStruct((col_count // 2, rows, width), t) for t in (BF16, F32)]
    found = pl.pallas_call(
        functools.partial(later_kernel, col_count, pieces, 2),
        in_specs=[HBM] * 2,
        out_specs=[HBM] * len(shapes),
        out_shape=[pltpu.HBM(shape.shape, shape.dtype) for shape in shapes],
        scratch_shapes=[
            pltpu.VMEM((pieces, rows * blocks, depth // pieces), BF16),
            pltpu.VMEM((pieces, depth // pieces, total), BF16),
            pltpu.VMEM((rows * blocks, total), F32),
            pltpu.VMEM((blocks, col_count // 2, rows, width), BF16),
            pltpu.VMEM((blocks, col_count // 2, rows, width), F32),
            pltpu.SemaphoreType.DMA((pieces, blocks)),
            pltpu.SemaphoreType.DMA((pieces,)),
            pltpu.SemaphoreType.DMA((len(shapes),)),
        ],
        compiler_params=params(60),
        cost_estimate=work(rows * blocks, depth, total),
    )(in_hbm(l_panel), in_hbm(after(x_solved, first[0])))
    halves = {target: found[2 * target - 2 : 2 * target] for target in range(1, steps)}

    def halve(target, stage, token):
        low, exact = halves[target]
        if stage:
            arrived_low = arrived[target]
            low, exact = combine(after(exact, token), arrived_low)
        else:
            low = after(low, token)
        pairs = [(i, i ^ (1 << stage)) for i in range(col_count)]
        halves[target] = (low, exact)
        arrived[target] = lax.ppermute(low, "col", pairs)


    def reduced(target, token, dtype):
        if target in chunks:
            own, parts = chunks[target][-1], arrived[target]
        else:
            own, parts = halves[target][1], [arrived[target]]
        return reduce_rows(rhs, target, after(own, token), parts, dtype)

    kept, other = reduced(0, (found[0], diag_other), BF16)
    halve(1, 0, other)
    resid_low = by_core(kept, swap(other), 0)
    results, solved_shards = [], {}
    products = {target: [] for target in range(steps)}
    stages = (col_count - 1).bit_length()
    diag_pick = [(diag_inv, diag_other, target) for target in range(steps)]
    inner_pick = [(l_inner, inner_other, index) for index in range(l_inner.shape[0])]
    near_matrix = {}
    for target in range(steps):
        last = target + 1 == steps
        shards = gather(resid_low, lower=last)
        if target == 0:
            diag_matrix, near_matrix[0] = load(resid_low, diag_pick[0], inner_pick[0])
            for stage in range(1, stages):
                halve(1, stage, diag_matrix)
        elif not last:
            diag_matrix, near_matrix[target] = load(
                resid_low, diag_pick[target], inner_pick[inner_index(target + 1, target)]
            )
            if target > 1:
                halve(target + 1, 0, resid_low)
            for stage in range(1, stages):
                halve(target + 1, stage, (resid_low, diag_matrix))
        else:
            (diag_matrix,) = load(resid_low, diag_pick[target])
            before = jnp.stack([other for _, other in results])
            swapped = swap(after(before, resid_low))
            parts = [by_core(kept, swapped[k], 1) for k, (kept, _) in enumerate(results)]
            solved = jnp.stack([*parts, jnp.zeros_like(parts[0])])
            shards[0], solved, diag_matrix = lax.optimization_barrier((shards[0], solved, diag_matrix))
        if last:
            kept, other = last_rows(diag_matrix, shards)
        else:
            kept, other, *low = apply_rows(diag_matrix, shards, [], 1, True, True)
        results.append((kept, other))
        if last:
            break
        (solved_low,) = low
        shards = gather(solved_low)
        solved_shards[target] = shards
        token = solved_low
        if target == 0:
            pass
        if target == 0:
            halve(target + 2, 0, token)
        kept, other = reduced(target + 1, token, F32)
        held = [(kept, swap(other))]
        if target:
            earlier = range(target)
            loaded = load(solved_low, *[inner_pick[inner_index(target + 1, k)] for k in earlier])
            for k, matrix in zip(earlier, loaded):
                held.append(apply_rows(matrix, solved_shards[k], [], 1, True, False))
        (resid_low,) = apply_rows(near_matrix[target], shards, held, -1, False, True)
    kept, other = results[-1]
    return lax.dynamic_update_slice(solved, by_core(kept, swap(other), 1)[None], (steps - 1, 0, 0))


def solution(mesh):
    in_specs = (
        P(None, "row", "col"),
        P(None, "row", "col"),
        P("col", None),
        P(None, "row", None),
        P(None, "row", None),
    )
    out_specs = P(None, "row", "col")
    body = functools.partial(local, row_count=mesh.shape["row"], col_count=mesh.shape["col"])
    return jax.shard_map(body, mesh=mesh, in_specs=in_specs, out_specs=out_specs, check_vma=False)
```
